256 devices in a mesh: row: 8 (over z), col: 32 (over y, x, core).
Axes of the slice: x: 4, y: 4, z: 8, core: 2. Of those that a mesh axis runs over, the one named last changes fastest.
Arguments:
- image_emb: bfloat16 [20480, 1152], P(('row', 'col')), may hold values from -0.19150809 to 0.19150809
- text_emb: bfloat16 [20480, 1152], P(('row', 'col')), may hold values from -0.19150809 to 0.19150809
- logit_scale: float32 [1], replicated, may hold values from 5 to 20
- logit_bias: float32 [1], replicated, may hold values from -6 to -1
Outputs:
- loss_rows: float32 [20480], P(('row', 'col'))
- image_grad: float32 [20480, 1152], P(('row', 'col'))
- text_grad: float32 [20480, 1152], P(('row', 'col'))
- scalar_grads: float32 [2], replicated
The draws below stay inside these ranges and needn't reach their ends.
All inputs are finite; a program needn't handle non-finite values.
Results may differ from the reference program's by a relative error of at most 0.00093.
Values may be sent and summed in bfloat16 or wider, within the bound.
No kernel may reach another device: no remote copies, remote signals or barrier semaphores. Data moves between devices by JAX's collectives and lax.ppermute only.
A program may use at most 64 MiB of HBM per device.

```python
import math
import jax
import jax.numpy as jnp
from jax import lax

D = 1152
TB = 640
IB = 2560
PAIRS = 20480
N_ROW = 8
N_COL = 32


def shared_direction(key):
    picked = jax.random.normal(jax.random.fold_in(key, 101), (D,), jnp.float32)
    return jnp.clip(picked, -4.0, 4.0) * D ** (-0.5)


def noise_rows(key):
    values = jnp.clip(jax.random.normal(key, (PAIRS, D), jnp.float32), -3.5, 3.5)
    return values * D ** (-0.5)


def draw_image_emb(key, part):
    direction = shared_direction(key)
    key = jax.random.fold_in(key, 3)
    amp = 0.6
    noise = noise_rows(key)
    index = jnp.arange(PAIRS, dtype=jnp.float32)
    rising = amp * (0.1 + index / PAIRS)
    return (noise + rising[:, None] * direction[None, :]).astype(jnp.bfloat16)


def draw_text_emb(key, part):
    direction = shared_direction(key)
    key = jax.random.fold_in(key, 5)
    index = jnp.arange(PAIRS, dtype=jnp.int32)
    column = (index // TB % N_COL).astype(jnp.float32)
    amp = 0.6
    noise = noise_rows(key)
    rising = amp * (0.1 + (column + 0.5) / N_COL)
    return (noise + rising[:, None] * direction[None, :]).astype(jnp.bfloat16)


def setup_inputs(seed: int = 0) -> dict:
    splits = jax.random.split(jax.random.key(seed), 5)
    image_emb = draw_image_emb(jax.random.fold_in(splits[4], 71), 0)
    text_emb = draw_text_emb(jax.random.fold_in(splits[4], 71), 0)
    logit_scale = jnp.clip(jnp.exp(jax.random.uniform(splits[2], (1,), jnp.float32, math.log(5.0), math.log(20.0))), 5.0, 20.0)
    logit_bias = jnp.clip(jax.random.uniform(splits[3], (1,), jnp.float32, -6.0, -1.0), -6.0, -1.0)
    return {"image_emb": image_emb, "text_emb": text_emb, "logit_scale": logit_scale, "logit_bias": logit_bias}


def normalize(emb):
    values = emb.astype(jnp.float32)
    inverse = lax.rsqrt(lax.optimization_barrier(jnp.sum(values * values, axis=1, keepdims=True)) + 1e-06)
    unit = values * inverse
    return (unit, inverse, unit.astype(jnp.bfloat16))

def reference(image_emb, text_emb, logit_scale, logit_bias):
    scale = logit_scale[0]
    bias = logit_bias[0]
    text_unit, text_inv, text_norm = normalize(text_emb)
    blocks = image_emb.reshape(N_ROW, IB, D)

    def step(carry, item):
        text_acc, sum_cos, sum_plain = carry
        block_id, block = item
        unit, inverse, normed = normalize(block)
        cosine = jnp.dot(normed, text_norm.T, preferred_element_type=jnp.float32)
        logits = scale * cosine + bias
        row_ids = block_id * IB + jnp.arange(IB, dtype=jnp.int32)
        col_ids = jnp.arange(PAIRS, dtype=jnp.int32)
        sign = jnp.where(row_ids[:, None] == col_ids[None, :], 1.0, -1.0).astype(jnp.float32)
        term = jax.nn.softplus(-sign * logits)
        loss_block = lax.optimization_barrier(jnp.sum(term, axis=1)) / PAIRS
        dlogit = -sign * jax.nn.sigmoid(-sign * logits)
        weights = (scale * dlogit).astype(jnp.bfloat16)
        image_g = jnp.dot(weights, text_norm, preferred_element_type=jnp.float32)
        text_acc = text_acc + jnp.dot(weights.T, normed, preferred_element_type=jnp.float32)
        grad_block = inverse * (image_g - unit * lax.optimization_barrier(jnp.sum(unit * image_g, axis=1, keepdims=True)))
        carry = (text_acc, sum_cos + jnp.sum(dlogit * cosine), sum_plain + jnp.sum(dlogit))
        return (carry, (loss_block, grad_block))
    start = (jnp.zeros((PAIRS, D), jnp.float32), jnp.zeros((), jnp.float32), jnp.zeros((), jnp.float32))
    (text_acc, sum_cos, sum_plain), (losses, grads) = lax.scan(step, start, (jnp.arange(N_ROW, dtype=jnp.int32), blocks))
    text_grad = text_inv * (text_acc - text_unit * lax.optimization_barrier(jnp.sum(text_unit * text_acc, axis=1, keepdims=True)))
    denom = jnp.float32(PAIRS) * jnp.float32(PAIRS)
    scalar_grads = jnp.stack([sum_cos, sum_plain]) / denom
    return (losses.reshape(PAIRS), grads.reshape(PAIRS, D), text_grad, scalar_grads)
```

```python
import jax
import jax.numpy as jnp
from jax import lax
from jax.experimental import pallas as pl
from jax.experimental.pallas import tpu as pltpu
from jax.sharding import PartitionSpec as P

NZ, NY, NX, NC = 8, 4, 4, 2
SHRINK = 0.125


def normalize(emb):
    values = emb.astype(jnp.float32)
    inverse = lax.rsqrt(jnp.sum(values * values, axis=1, keepdims=True) + 1e-06)
    unit = values * inverse
    return (unit, inverse, unit.astype(jnp.bfloat16))


def send_z(x, d):
    return lax.ppermute(x, "row", [(i, (i + d) % NZ) for i in range(NZ)])


def send_plane(x, dy, dx, dc):
    pairs = []
    for y in range(NY):
        for x_ in range(NX):
            for c in range(NC):
                src = (y * NX + x_) * NC + c
                dst = (((y + dy) % NY) * NX + (x_ + dx) % NX) * NC + (c + dc) % NC
                pairs.append((src, dst))
    return lax.ppermute(x, "col", pairs)


def send_y(x, d):
    return send_plane(x, d, 0, 0)


def send_x(x, d):
    return send_plane(x, 0, d, 0)


def swap(x):
    return send_plane(x, 0, 0, 1)


def narrow(x):
    return (x * SHRINK).astype(jnp.float16)


def widen(x):
    return x.astype(jnp.float32) * (1.0 / SHRINK)


def pair_kernel(own, total, sc_ref, img_ref, txt_ref, gi_ref, gt_ref, loss_ref, sums_ref):
    step = pl.program_id(0)
    scale = sc_ref[0]
    bias = sc_ref[1]
    img = img_ref[...]
    txt = txt_ref[...]
    rows, cols = img.shape[0], txt.shape[0]
    cosine = lax.dot_general(
        img, txt, (((1,), (1,)), ((), ())), preferred_element_type=jnp.float32
    )
    logits = scale * cosine + bias
    half = own // 2
    r = lax.broadcasted_iota(jnp.int32, (rows, 128), 0) + step * rows
    c = lax.broadcasted_iota(jnp.int32, (rows, 128), 1)
    split = (pl.num_programs(0) * rows) // 2
    match = ((r == c) & (r < half)) | ((r - split == c - half) & (c >= half) & (c < own))
    sign = jnp.where(match, -1.0, 1.0)
    head = sign * logits[:, :128]
    signed = jnp.concatenate([head, logits[:, 128:]], axis=1)
    e = jnp.exp(signed)
    p = 1.0 + e
    d = e / p
    d = jnp.concatenate([sign * d[:, :128], d[:, 128:]], axis=1)
    acc = None
    k = 0
    while k < cols:
        q = p[:, k : k + 128]
        for m in range(1, 4):
            if k + 128 * m < cols:
                q = q * p[:, k + 128 * m : k + 128 * (m + 1)]
        q = jnp.log(q)
        acc = q if acc is None else acc + q
        k += 512
    loss_ref[...] = jnp.sum(acc, axis=1, keepdims=True) / total
    sums = jnp.concatenate(
        [
            jnp.sum(d * cosine, axis=0, keepdims=True),
            jnp.sum(d, axis=0, keepdims=True),
        ],
        axis=0,
    )
    w = (scale * d).astype(jnp.bfloat16)
    gi_ref[...] = jnp.dot(w, txt, preferred_element_type=jnp.float32)
    gt = lax.dot_general(w, img, (((0,), (0,)), ((), ())), preferred_element_type=jnp.float32)

    @pl.when(step == 0)
    def _():
        gt_ref[...] = gt
        sums_ref[...] = sums

    @pl.when(step > 0)
    def _():
        gt_ref[...] += gt
        sums_ref[...] += sums


def pairs_block(images, texts, scale, bias, own, total):
    rows, width = images.shape
    cols = texts.shape[0]
    tile = rows // 5
    return pl.pallas_call(
        lambda *refs: pair_kernel(own, total, *refs),
        grid=(rows // tile,),
        in_specs=[
            pl.BlockSpec(memory_space=pltpu.SMEM),
            pl.BlockSpec((tile, width), lambda i: (i, 0)),
            pl.BlockSpec((cols, width), lambda i: (0, 0)),
        ],
        out_specs=[
            pl.BlockSpec((tile, width), lambda i: (i, 0)),
            pl.BlockSpec((cols, width), lambda i: (0, 0)),
            pl.BlockSpec((tile, 1), lambda i: (i, 0)),
            pl.BlockSpec((2, cols), lambda i: (0, 0)),
        ],
        out_shape=[
            jax.ShapeDtypeStruct((rows, width), jnp.float32),
            jax.ShapeDtypeStruct((cols, width), jnp.float32),
            jax.ShapeDtypeStruct((rows, 1), jnp.float32),
            jax.ShapeDtypeStruct((2, cols), jnp.float32),
        ],
        compiler_params=pltpu.CompilerParams(vmem_limit_bytes=48 * 1024 * 1024),
        name="pair_block",
    )(jnp.stack([scale, bias]), images, texts)


def body(image_emb, text_emb, logit_scale, logit_bias):
    scale = logit_scale[0]
    bias = logit_bias[0]
    own = text_emb.shape[0]
    half = own // 2
    total_pairs = own * NZ * NY * NX * NC
    image_unit, image_inv, image_local = normalize(image_emb)
    text_unit, text_inv, text_local = normalize(text_emb)

    t_up = send_z(text_local, -1)
    t_down = send_z(text_local, 1)
    t_far = send_z(text_local, 4)
    a = image_local[:half]
    b = image_local[half:]
    a1 = jnp.concatenate([a] + [send_y(a, -i) for i in range(1, NY)], axis=0)
    b1 = jnp.concatenate([b] + [send_x(b, -i) for i in range(1, NX)], axis=0)
    t_up2 = send_z(jnp.concatenate([t_up, t_far], axis=0), -1)
    t_down2 = send_z(jnp.concatenate([t_down, t_far], axis=0), 1)
    a2 = [a1] + [send_x(a1, -i) for i in range(1, NX)]
    b2 = [b1] + [send_y(b1, -i) for i in range(1, NY)]
    texts_core = jnp.concatenate([text_local, t_up, t_down, t_far, t_up2, t_down2], axis=0)
    texts = jnp.concatenate([texts_core, swap(texts_core)], axis=0)
    images = jnp.concatenate(a2 + b2, axis=0)

    gi, gt, loss, sums = pairs_block(images, texts, scale, bias, own, float(total_pairs))

    sums = lax.psum(jnp.sum(sums, axis=1), ("row", "col"))
    denom = jnp.float32(total_pairs) * jnp.float32(total_pairs)
    scalar_grads = sums / denom

    n = own * NZ
    gt_core = gt[:n] + widen(swap(narrow(gt[n:])))
    pieces = [gt_core[i * own : (i + 1) * own] for i in range(NZ)]
    up = send_z(narrow(jnp.concatenate([pieces[4], pieces[5]], axis=0)), 1)
    down = send_z(narrow(jnp.concatenate([pieces[6], pieces[7]], axis=0)), -1)
    up = widen(up)
    down = widen(down)
    p_up = pieces[1] + up[:own]
    p_down = pieces[2] + down[:own]
    p_far = pieces[3] + up[own:] + down[own:]
    text_share = (
        pieces[0]
        + widen(send_z(narrow(p_up), 1))
        + widen(send_z(narrow(p_down), -1))
        + widen(send_z(narrow(p_far), 4))
    )

    def reduce_two(g, first, second):
        g = g.reshape(4, 4 * half, g.shape[1])
        s = g[0]
        for i in range(1, 4):
            s = s + widen(first(narrow(g[i]), i))
        s = s.reshape(4, half, g.shape[2])
        t = s[0]
        for i in range(1, 4):
            t = t + widen(second(narrow(s[i]), i))
        return t

    m = gi.shape[0] // 2
    image_share = jnp.concatenate(
        [reduce_two(gi[:m], send_x, send_y), reduce_two(gi[m:], send_y, send_x)], axis=0
    )
    la = loss[:m, 0].reshape(NX, NY, half)
    lb = loss[m:, 0].reshape(NY, NX, half)
    col = lax.axis_index("col")
    y0 = col // (NX * NC)
    x0 = col // NC % NX
    c0 = col % NC
    la = jnp.roll(la.transpose(1, 0, 2), (y0, x0), (0, 1))
    lb = jnp.roll(lb, (y0, x0), (0, 1))
    both = jnp.concatenate([la, lb], axis=2)
    both = jnp.where(
        jnp.arange(NC)[None, None, :, None] == c0, both[:, :, None, :], 0.0
    ).reshape(-1)
    loss_rows = lax.psum_scatter(both, "col", scatter_dimension=0, tiled=True)

    text_grad = text_inv * (
        text_share - text_unit * jnp.sum(text_unit * text_share, axis=1, keepdims=True)
    )
    image_grad = image_inv * (
        image_share - image_unit * jnp.sum(image_unit * image_share, axis=1, keepdims=True)
    )
    return (loss_rows, image_grad, text_grad, scalar_grads)


def solution(mesh):
    return jax.shard_map(
        body,
        mesh=mesh,
        in_specs=(P(("row", "col"), None), P(("row", "col"), None), P(), P()),
        out_specs=(P(("row", "col")), P(("row", "col"), None), P(("row", "col"), None), P()),
        check_vma=False,
    )
```

```python
import math
import jax
import jax.numpy as jnp
from jax import lax
from jax.experimental import pallas as pl
from jax.experimental.pallas import tpu as pltpu
from jax.sharding import PartitionSpec as P

NZ, NY, NX, NC = 8, 4, 4, 2
SHRINK = 0.125
LOG2E = 1.0 / math.log(2.0)


def send_z(x, d):
    return lax.ppermute(x, "row", [(i, (i + d) % NZ) for i in range(NZ)])


def send_plane(x, move):
    pairs = []
    for y in range(NY):
        for x_ in range(NX):
            for c in range(NC):
                dy, dx, dc = move(c)
                src = (y * NX + x_) * NC + c
                dst = (((y + dy) % NY) * NX + (x_ + dx) % NX) * NC + (c + dc) % NC
                pairs.append((src, dst))
    return lax.ppermute(x, "col", pairs)


def send_light(x, i):
    return send_plane(x, lambda c: (i, 0, 0) if c == 0 else (0, i, 0))


def send_heavy(x, i):
    return send_plane(x, lambda c: (0, i, 0) if c == 0 else (i, 0, 0))


def swap(x):
    return send_plane(x, lambda c: (0, 0, 1))


def after(x, y):
    return x + 0.0 * y[:1, :128].astype(jnp.float32)


def narrow(x):
    return (x * SHRINK).astype(jnp.float16)


def widen(x):
    return x.astype(jnp.float32) * (1.0 / SHRINK)


def join_kernel(groups, count, *refs):
    ins, outs = refs[:count], refs[count:]
    for out, group in zip(outs, groups):
        at = 0
        for k in group:
            rows = ins[k].shape[0]
            out[at : at + rows, :] = ins[k][...]
            at += rows


def join(arrays, groups, name):
    vmem = pl.BlockSpec(memory_space=pltpu.VMEM)
    width = arrays[0].shape[1]
    return pl.pallas_call(
        lambda *refs: join_kernel(groups, len(arrays), *refs),
        in_specs=[vmem] * len(arrays),
        out_specs=[vmem] * len(groups),
        out_shape=[
            jax.ShapeDtypeStruct((sum(arrays[k].shape[0] for k in g), width), arrays[0].dtype)
            for g in groups
        ],
        compiler_params=pltpu.CompilerParams(vmem_limit_bytes=16 * 1024 * 1024),
        name=name,
    )(*arrays)


def weights_kernel(
    sc_ref, i0, i1, i2, i3, t0, t1,
    w_ref, loss_ref, sums_ref, i_out, t_out,
    img, txt, sem_i, sem_t, sem_io, sem_to,
):
    images = (i0, i1, i2, i3)
    halves = (t0, t1)
    n = i0.shape[0]
    m = t0.shape[0]
    ins = [pltpu.make_async_copy(halves[k], txt.at[pl.ds(k * m, m)], sem_t.at[k]) for k in range(2)]
    ins += [pltpu.make_async_copy(images[k], img.at[pl.ds(k * n, n)], sem_i.at[k]) for k in range(4)]
    outs = [pltpu.make_async_copy(txt.at[pl.ds(k * m, m)], t_out.at[pl.ds(k * m, m)], sem_to.at[k]) for k in range(2)]
    outs += [pltpu.make_async_copy(img.at[pl.ds(k * n, n)], i_out.at[pl.ds(k * n, n)], sem_io.at[k]) for k in range(4)]
    for c in ins:
        c.start()
    for c in ins:
        c.wait()
    for c in outs:
        c.start()

    scale = sc_ref[0]
    a = sc_ref[1]
    b = sc_ref[2]
    per_pair = sc_ref[3]
    rows = img[...]
    total, cols = img.shape[0], txt.shape[0]
    wide = 256
    log_sum = None
    product = None
    sum_d = None
    sum_dc = None
    for k in range(cols // wide):
        cosine = lax.dot_general(
            rows, txt[k * wide : (k + 1) * wide, :], (((1,), (1,)), ((), ())),
            preferred_element_type=jnp.float32,
        )
        e = jnp.exp2(cosine * a + b)
        p = 1.0 + e
        r = pltpu.reciprocal(p, approx=True)
        r = r * (2.0 - p * r)
        d = e * r
        w_ref[:, k * wide : (k + 1) * wide] = (scale * d).astype(jnp.bfloat16)
        q = jnp.log(p[:, :128] * p[:, 128:])
        log_sum = q if log_sum is None else log_sum + q
        dc = d * cosine
        d = jnp.sum((d[:, :128] + d[:, 128:]).reshape(total // 8, 8, 128), axis=0)
        dc = jnp.sum((dc[:, :128] + dc[:, 128:]).reshape(total // 8, 8, 128), axis=0)
        sum_d = d if sum_d is None else sum_d + d
        sum_dc = dc if sum_dc is None else sum_dc + dc
    loss_ref[...] = jnp.sum(log_sum, axis=1, keepdims=True) * per_pair
    sums_ref[0] = sum_dc
    sums_ref[1] = sum_d
    for c in outs:
        c.wait()


def weights_block(scalars, images, texts):
    n, width = images[0].shape
    cols = 2 * texts[0].shape[0]
    rows = 4 * n
    anywhere = pl.BlockSpec(memory_space=pl.ANY)
    return pl.pallas_call(
        weights_kernel,
        in_specs=[pl.BlockSpec(memory_space=pltpu.SMEM)] + [anywhere] * 6,
        out_specs=[pl.BlockSpec(memory_space=pltpu.VMEM)] * 3 + [anywhere] * 2,
        out_shape=[
            jax.ShapeDtypeStruct((rows, cols), jnp.bfloat16),
            jax.ShapeDtypeStruct((rows, 1), jnp.float32),
            jax.ShapeDtypeStruct((2, 8, 128), jnp.float32),
            jax.ShapeDtypeStruct((rows, width), jnp.bfloat16),
            jax.ShapeDtypeStruct((cols, width), jnp.bfloat16),
        ],
        scratch_shapes=[
            pltpu.VMEM((rows, width), jnp.bfloat16),
            pltpu.VMEM((cols, width), jnp.bfloat16),
            pltpu.SemaphoreType.DMA((4,)),
            pltpu.SemaphoreType.DMA((2,)),
            pltpu.SemaphoreType.DMA((4,)),
            pltpu.SemaphoreType.DMA((2,)),
        ],
        compiler_params=pltpu.CompilerParams(vmem_limit_bytes=40 * 1024 * 1024),
        name="pair_weights",
    )(scalars, *images, *texts)


def norm_kernel(i_ref, t_ref, in_ref, tn_ref, ii_ref, ti_ref):
    for src, out, inv in ((i_ref, in_ref, ii_ref), (t_ref, tn_ref, ti_ref)):
        values = src[...].astype(jnp.float32)
        inverse = lax.rsqrt(jnp.sum(values * values, axis=1, keepdims=True) + 1e-06)
        out[...] = (values * inverse).astype(jnp.bfloat16)
        inv[...] = inverse


def normalize_both(image_emb, text_emb):
    rows, width = image_emb.shape
    vmem = pl.BlockSpec(memory_space=pltpu.VMEM)
    return pl.pallas_call(
        norm_kernel,
        in_specs=[vmem] * 2,
        out_specs=[vmem] * 4,
        out_shape=[jax.ShapeDtypeStruct((rows, width), jnp.bfloat16)] * 2
        + [jax.ShapeDtypeStruct((rows, 1), jnp.float32)] * 2,
        name="normalize",
    )(image_emb, text_emb)


def body(image_emb, text_emb, logit_scale, logit_bias):
    scale = logit_scale[0]
    bias = logit_bias[0]
    own = text_emb.shape[0]
    total = own * NZ * NY * NX * NC
    z0 = lax.axis_index("row")
    col = lax.axis_index("col")
    y0 = col // (NX * NC)
    x0 = col // NC % NX
    c0 = col % NC

    image_local, text_local, image_inv, text_inv = normalize_both(image_emb, text_emb)

    near = [image_local] + [send_light(image_local, -i) for i in range(1, 4)]
    t_up = send_z(text_local, -1)
    t_down = send_z(text_local, 1)
    t_far = send_z(text_local, 4)
    near, m_up, m_down = join(
        near + [t_up, t_down, t_far], [(0, 1, 2, 3), (4, 6), (5, 6)], "join_first"
    )
    images = [near] + [send_heavy(near, -i) for i in (1, 3, 2)]
    images = [images[0], images[1], images[3], images[2]]
    t_up2 = send_z(m_up, -1)
    t_down2 = send_z(m_down, 1)
    (texts,) = join(
        [text_local, t_up, t_down, t_far, t_up2, t_down2], [(0, 1, 2, 3, 4, 5)], "join_texts"
    )
    scalars = jnp.stack([scale, scale * LOG2E, bias * LOG2E, jnp.float32(1.0 / total)])
    w, loss, sums, img, txt = weights_block(scalars, images, [texts, swap(texts)])

    k = jnp.arange(NY * NX, dtype=jnp.int32)
    first = (k // NX - y0) % NY
    second = (k % NX - x0) % NX
    place = jnp.where(c0 == 0, second * 4 + first, first * 4 + second)
    blocks = loss.reshape(NY * NX, own)
    placed = jnp.sum(
        jnp.where(place[:, None, None] == k[None, :, None], blocks[None], 0.0), axis=1
    )
    image_f = image_local.astype(jnp.float32)
    text_f = text_local.astype(jnp.float32)
    cosine = jnp.sum(image_f * text_f, axis=1, keepdims=True)
    logits = scale * cosine + bias
    extra = jnp.stack([jnp.sum(cosine), jnp.float32(own)])
    totals = jnp.sum(sums, axis=(1, 2)) - extra
    small = jnp.concatenate([placed.reshape(-1), totals, jnp.zeros((126,), jnp.float32)])
    small = small.reshape(-1, 128)
    for d in (1, 2):
        small = small + send_light(small, d)
    for d in (1, 2):
        small = small + send_heavy(small, d)
    mine = y0 * NX + x0
    loss_sum = lax.dynamic_slice(small.reshape(-1), (mine * own,), (own,))
    tail = small[-1:]

    n = own * NZ
    contract = (((0,), (0,)), ((), ()))
    theirs = narrow(
        lax.dot_general(w[:, n:], img, contract, preferred_element_type=jnp.float32)
    )
    theirs = swap(theirs)
    tail = after(tail, theirs)
    tail = tail + send_z(tail, 1)
    gt = lax.dot_general(w[:, :n], img, contract, preferred_element_type=jnp.float32)
    gt = gt + widen(theirs)
    pieces = [gt[i * own : (i + 1) * own] for i in range(NZ)]
    up = widen(send_z(narrow(gt[4 * own : 6 * own]), 1))
    down = widen(send_z(narrow(gt[6 * own : 8 * own]), -1))
    tail = after(tail, up)
    tail = tail + send_z(tail, 2)
    p_up = pieces[1] + up[:own]
    p_down = pieces[2] + down[:own]
    p_far = pieces[3] + up[own:] + down[own:]
    text_share = (
        pieces[0]
        + widen(send_z(narrow(p_up), 1))
        + widen(send_z(narrow(p_down), -1))
        + widen(send_z(narrow(p_far), 4))
    )

    m = 4 * own
    got = []
    for i in range(1, 4):
        part = jnp.dot(w[i * m : (i + 1) * m], txt, preferred_element_type=jnp.float32)
        got.append(send_heavy(narrow(part), i))
    part = jnp.dot(w[:m], txt, preferred_element_type=jnp.float32)
    for g in got:
        part = part + widen(g)
    image_share = part[:own]
    for i in range(1, 4):
        image_share = image_share + widen(
            send_light(narrow(part[i * own : (i + 1) * own]), i)
        )

    tail = tail + send_z(tail, 4)
    tail = tail + swap(tail)

    d = jax.nn.sigmoid(logits)
    w_plain = (scale * d).astype(jnp.bfloat16).astype(jnp.float32)
    w_right = (scale * -jax.nn.sigmoid(-logits)).astype(jnp.bfloat16).astype(jnp.float32)
    fix = w_right - w_plain
    image_share = image_share + fix * text_f
    text_share = text_share + fix * image_f
    loss_rows = loss_sum - logits[:, 0] / total
    denom = jnp.float32(total) * jnp.float32(total)
    scalar_grads = tail[0, :2] / denom

    image_unit = image_emb.astype(jnp.float32) * image_inv
    text_unit = text_emb.astype(jnp.float32) * text_inv
    text_grad = text_inv * (
        text_share - text_unit * jnp.sum(text_unit * text_share, axis=1, keepdims=True)
    )
    image_grad = image_inv * (
        image_share - image_unit * jnp.sum(image_unit * image_share, axis=1, keepdims=True)
    )
    return (loss_rows, image_grad, text_grad, scalar_grads)


def solution(mesh):
    return jax.shard_map(
        body,
        mesh=mesh,
        in_specs=(P(("row", "col"), None), P(("row", "col"), None), P(), P()),
        out_specs=(P(("row", "col")), P(("row", "col"), None), P(("row", "col"), None), P()),
        check_vma=False,
    )
```

```python
import math
import jax
import jax.numpy as jnp
from jax import lax
from jax.experimental import pallas as pl
from jax.experimental.pallas import tpu as pltpu
from jax.sharding import PartitionSpec as P

NZ, NY, NX, NC = 8, 4, 4, 2
SHRINK = 0.125
LOG2E = 1.0 / math.log(2.0)
EXTRA = 128
LIFT = 1024.0


def send_z(x, d):
    return lax.ppermute(x, "row", [(i, (i + d) % NZ) for i in range(NZ)])


def send_ring(x, d):
    pairs = []
    for z in range(NZ):
        for s in range(NY * NX):
            for c in range(NC):
                to = (z + (d if c == 0 else -d)) % NZ
                pairs.append(((z * NY * NX + s) * NC + c, (to * NY * NX + s) * NC + c))
    return lax.ppermute(x, ("row", "col"), pairs)


def send_plane(x, move):
    pairs = []
    for y in range(NY):
        for x_ in range(NX):
            for c in range(NC):
                dy, dx, dc = move(c)
                src = (y * NX + x_) * NC + c
                dst = (((y + dy) % NY) * NX + (x_ + dx) % NX) * NC + (c + dc) % NC
                pairs.append((src, dst))
    return lax.ppermute(x, "col", pairs)


def send_light(x, i):
    return send_plane(x, lambda c: (i, 0, 0) if c == 0 else (0, i, 0))


def send_heavy(x, i):
    return send_plane(x, lambda c: (0, i, 0) if c == 0 else (i, 0, 0))


def swap(x):
    return send_plane(x, lambda c: (0, 0, 1))


def narrow(x, tail=None):
    x = x * SHRINK
    if tail is not None:
        x = x + 0.0 * tail[0, 0]
    return x.astype(jnp.float16)


def widen(x):
    return x.astype(jnp.float32) * (1.0 / SHRINK)


def join_kernel(groups, count, *refs):
    ins, outs = refs[:count], refs[count:]
    for out, group in zip(outs, groups):
        at = 0
        for k in group:
            rows = ins[k].shape[0]
            out[at : at + rows, :] = ins[k][...]
            at += rows


def join(arrays, groups, name, later=()):
    vmem = pl.BlockSpec(memory_space=pltpu.VMEM)
    width = arrays[0].shape[1]
    return pl.pallas_call(
        lambda *refs: join_kernel(
            groups, len(arrays), *refs[: len(arrays)], *refs[len(arrays) + len(later) :]
        ),
        in_specs=[vmem] * len(arrays) + [pl.BlockSpec(memory_space=pl.ANY)] * len(later),
        out_specs=[vmem] * len(groups),
        out_shape=[
            jax.ShapeDtypeStruct((sum(arrays[k].shape[0] for k in g), width), arrays[0].dtype)
            for g in groups
        ],
        compiler_params=pltpu.CompilerParams(vmem_limit_bytes=16 * 1024 * 1024),
        name=name,
    )(*arrays, *later)


def weights_kernel(
    sc_ref, i0, i1, i2, i3, x0, t1, t2, t3, t4, t5, t6, t7, t8,
    w, img, txt, sums_ref, sem_i, sem_t,
):
    n, width = i0.shape
    own = t1.shape[0]
    mine, other = x0.at[pl.ds(0, own)], x0.at[pl.ds(own, own)]
    texts = (mine, t1, t2, t3, t4, other, t5, t6, t7, t8)
    total, cols = 4 * n, 16 * own
    ins_i = [
        pltpu.make_async_copy(ref, img.at[pl.ds(k * n, n)], sem_i.at[k])
        for k, ref in enumerate((i0, i1, i2, i3))
    ]
    ins_t = []
    at = 0
    for k, ref in enumerate(texts):
        rows = ref.shape[0]
        ins_t.append(
            pltpu.make_async_copy(
                ref, txt.at[pl.ds(at, rows), pl.ds(0, width)], sem_t.at[k]
            )
        )
        at += rows
    for c in ins_i + ins_t:
        c.start()
    txt[:cols, width:] = jnp.zeros((cols, EXTRA), jnp.bfloat16)
    txt[cols:, :width] = jnp.zeros((EXTRA, width), jnp.bfloat16)
    r = lax.broadcasted_iota(jnp.int32, (EXTRA, EXTRA), 0)
    c = lax.broadcasted_iota(jnp.int32, (EXTRA, EXTRA), 1)
    txt[cols:, width:] = jnp.where(r == c, 1.0, 0.0).astype(jnp.bfloat16)
    for c in ins_i + ins_t:
        c.wait()

    scale = sc_ref[0]
    a = sc_ref[1]
    b = sc_ref[2]
    lift = sc_ref[3]
    rows = img[...]
    wide = 256
    log_sum = None
    sum_d = None
    sum_dc = None
    for k in range(cols // wide):
        lo, hi = k * wide, (k + 1) * wide
        cosine = lax.dot_general(
            rows, txt[lo:hi, :width], (((1,), (1,)), ((), ())),
            preferred_element_type=jnp.float32,
        )
        e = jnp.exp2(cosine * a + b)
        p = 1.0 + e
        r = pltpu.reciprocal(p, approx=True)
        r = r * (2.0 - p * r)
        d = e * r
        w[:, lo:hi] = (scale * d).astype(jnp.bfloat16)
        q = jnp.log(p[:, :128] * p[:, 128:])
        log_sum = q if log_sum is None else log_sum + q
        dc = d * cosine
        d = jnp.sum((d[:, :128] + d[:, 128:]).reshape(total // 8, 8, 128), axis=0)
        dc = jnp.sum((dc[:, :128] + dc[:, 128:]).reshape(total // 8, 8, 128), axis=0)
        sum_d = d if sum_d is None else sum_d + d
        sum_dc = dc if sum_dc is None else sum_dc + dc
    loss = jnp.sum(log_sum, axis=1, keepdims=True) * lift
    high = loss.astype(jnp.bfloat16).astype(jnp.float32)
    lane = lax.broadcasted_iota(jnp.int32, (total, EXTRA), 1)
    w[:, cols:] = jnp.where(
        lane == 0, high, jnp.where(lane == 1, loss - high, 0.0)
    ).astype(jnp.bfloat16)
    sums_ref[0] = sum_dc
    sums_ref[1] = sum_d


def weights_block(scalars, images, texts):
    n, width = images[0].shape
    rows = 4 * n
    cols = sum(t.shape[0] for t in texts)
    vmem = pl.BlockSpec(memory_space=pltpu.VMEM)
    return pl.pallas_call(
        weights_kernel,
        in_specs=[pl.BlockSpec(memory_space=pltpu.SMEM)]
        + [pl.BlockSpec(memory_space=pltpu.HBM)] * 13,
        out_specs=[vmem] * 4,
        out_shape=[
            pltpu.VMEM((rows, cols + EXTRA), jnp.bfloat16),
            pltpu.VMEM((rows, width), jnp.bfloat16),
            pltpu.VMEM((cols + EXTRA, width + EXTRA), jnp.bfloat16),
            jax.ShapeDtypeStruct((2, 8, 128), jnp.float32),
        ],
        scratch_shapes=[pltpu.SemaphoreType.DMA((4,)), pltpu.SemaphoreType.DMA((10,))],
        compiler_params=pltpu.CompilerParams(vmem_limit_bytes=32 * 1024 * 1024),
        name="pair_weights",
    )(scalars, *images, *texts)


def normal(ref):
    values = ref[...].astype(jnp.float32)
    inverse = lax.rsqrt(jnp.sum(values * values, axis=1, keepdims=True) + 1e-06)
    return (values * inverse).astype(jnp.bfloat16), inverse


def norm_kernel(i_ref, t_ref, in_ref, tn_ref, ii_ref, ti_ref):
    in_ref[...], ii_ref[...] = normal(i_ref)
    tn_ref[...], ti_ref[...] = normal(t_ref)


def normalize_both(image_emb, text_emb):
    rows, width = image_emb.shape
    vmem = pl.BlockSpec(memory_space=pltpu.VMEM)
    return pl.pallas_call(
        norm_kernel,
        in_specs=[vmem] * 2,
        out_specs=[vmem] * 4,
        out_shape=[jax.ShapeDtypeStruct((rows, width), jnp.bfloat16)] * 2
        + [jax.ShapeDtypeStruct((rows, 1), jnp.float32)] * 2,
        name="normalize",
    )(image_emb, text_emb)


def shard_kernel(tn_ref, o_ref, out):
    own = tn_ref.shape[0]
    out[:own, :] = tn_ref[...]
    out[own:, :] = normal(o_ref)[0]


def chip_shard(text_local, other_emb):
    rows, width = text_local.shape
    vmem = pl.BlockSpec(memory_space=pltpu.VMEM)
    return pl.pallas_call(
        shard_kernel,
        in_specs=[vmem] * 2,
        out_specs=vmem,
        out_shape=jax.ShapeDtypeStruct((2 * rows, width), jnp.bfloat16),
        name="chip_shard",
    )(text_local, other_emb)


def body(image_emb, text_emb, logit_scale, logit_bias):
    scale = logit_scale[0]
    bias = logit_bias[0]
    own = text_emb.shape[0]
    total = own * NZ * NY * NX * NC
    image_local, text_local, image_inv, text_inv = normalize_both(image_emb, text_emb)

    shard = chip_shard(text_local, swap(text_emb))
    ring1 = send_ring(shard, 1)
    near = [image_local] + [send_light(image_local, -i) for i in range(1, 4)]
    (near,) = join(near, [(0, 1, 2, 3)], "join_near")
    images = [near] + [send_heavy(near, -i) for i in (1, 3, 2)]
    images = [images[0], images[1], images[3], images[2]]
    ring2 = send_ring(ring1, 1)
    ring3 = send_ring(ring2, 1)
    ring4 = send_ring(ring3[:own], 1)
    scalars = jnp.stack([scale, scale * LOG2E, bias * LOG2E, jnp.float32(LIFT / total)])
    w, img, txt, sums = weights_block(
        scalars, images,
        [shard, ring4, ring1, ring2, ring3]
        + [swap(ring4), swap(ring1), swap(ring2), swap(ring3)],
    )

    image_f = image_local.astype(jnp.float32)
    text_f = text_local.astype(jnp.float32)
    cosine = jnp.sum(image_f * text_f, axis=1, keepdims=True)
    logits = scale * cosine + bias
    width = image_f.shape[1]
    square = jnp.float32(total) * jnp.float32(total)
    extra = jnp.stack([jnp.sum(cosine), jnp.float32(own)])
    tail = (jnp.sum(sums, axis=(1, 2)) - extra) * (1.0 / square)
    tail = jnp.pad(tail, (0, 126)).reshape(1, 128)
    n = own * NZ
    m = 4 * own
    contract = (((0,), (0,)), ((), ()))

    def heavy(i, tail):
        part = jnp.dot(w[i * m : (i + 1) * m], txt, preferred_element_type=jnp.float32)
        return send_heavy(narrow(part, tail), i)

    theirs = lax.dot_general(w[:, n : 2 * n], img, contract, preferred_element_type=jnp.float32)
    theirs = swap(narrow(theirs))
    tail = tail + swap(tail)
    got = [heavy(1, tail)]
    tail = tail + send_z(tail, 1)
    gt = lax.dot_general(w[:, :n], img, contract, preferred_element_type=jnp.float32)
    gt = gt + widen(theirs)
    back2 = widen(send_ring(narrow(gt[m:]), -2))
    back_far = send_z(narrow(gt[own : 2 * own]), 4)
    got.append(heavy(3, tail))
    tail = tail + 0.0 * gt[0, 0]
    tail = tail + send_z(tail, 2)
    got.append(heavy(2, tail))
    tail = tail + send_z(tail, 4)
    for d in (1, 2):
        tail = tail + send_heavy(tail, d)
    back1 = widen(send_ring(narrow(gt[2 * own : m] + back2[2 * own :]), -1))
    back0 = back2[: 2 * own] + back1
    text_share = gt[:own] + widen(back_far) + back0[:own] + widen(swap(narrow(back0[own:])))

    part = jnp.dot(w[:m], txt, preferred_element_type=jnp.float32)
    for g in got:
        part = part + widen(g)
    part = part + jnp.pad(tail[:, :2] * LIFT, ((0, 0), (width + 2, EXTRA - 4)))
    image_share = part[:own]
    for i in range(1, 4):
        image_share = image_share + widen(
            send_light(narrow(part[i * own : (i + 1) * own]), i)
        )
    side = image_share[:, width:] * (1.0 / LIFT)
    image_share = image_share[:, :width]
    loss_sum = side[:, 0] + side[:, 1]
    scalar_grads = side[0, 2:4]

    d = jax.nn.sigmoid(logits)
    w_plain = (scale * d).astype(jnp.bfloat16).astype(jnp.float32)
    w_right = (scale * -jax.nn.sigmoid(-logits)).astype(jnp.bfloat16).astype(jnp.float32)
    fix = w_right - w_plain
    image_share = image_share + fix * text_f
    text_share = text_share + fix * image_f
    loss_rows = loss_sum - logits[:, 0] / total
    image_unit = image_emb.astype(jnp.float32) * image_inv
    text_unit = text_emb.astype(jnp.float32) * text_inv
    text_grad = text_inv * (
        text_share - text_unit * jnp.sum(text_unit * text_share, axis=1, keepdims=True)
    )
    image_grad = image_inv * (
        image_share - image_unit * jnp.sum(image_unit * image_share, axis=1, keepdims=True)
    )
    return (loss_rows, image_grad, text_grad, scalar_grads)


def solution(mesh):
    return jax.shard_map(
        body,
        mesh=mesh,
        in_specs=(P(("row", "col"), None), P(("row", "col"), None), P(), P()),
        out_specs=(P(("row", "col")), P(("row", "col"), None), P(("row", "col"), None), P()),
        check_vma=False,
    )
```

```python
import functools
import math
import jax
import jax.numpy as jnp
from jax import lax
from jax.experimental import pallas as pl
from jax.experimental.pallas import tpu as pltpu
from jax.sharding import PartitionSpec as P

NZ, NY, NX, NC = 8, 4, 4, 2
SHRINK = 0.125
LOG2E = 1.0 / math.log(2.0)
EXTRA = 128
LIFT = 1024.0


def send_z(x, d):
    return lax.ppermute(x, "row", [(i, (i + d) % NZ) for i in range(NZ)])


def send_ring(x, d):
    pairs = []
    for z in range(NZ):
        for s in range(NY * NX):
            for c in range(NC):
                to = (z + (d if c == 0 else -d)) % NZ
                pairs.append(((z * NY * NX + s) * NC + c, (to * NY * NX + s) * NC + c))
    return lax.ppermute(x, ("row", "col"), pairs)


def send_plane(x, move):
    pairs = []
    for y in range(NY):
        for x_ in range(NX):
            for c in range(NC):
                dy, dx, dc = move(c)
                src = (y * NX + x_) * NC + c
                dst = (((y + dy) % NY) * NX + (x_ + dx) % NX) * NC + (c + dc) % NC
                pairs.append((src, dst))
    return lax.ppermute(x, "col", pairs)


def send_light(x, i):
    return send_plane(x, lambda c: (i, 0, 0) if c == 0 else (0, i, 0))


def send_heavy(x, i):
    return send_plane(x, lambda c: (0, i, 0) if c == 0 else (i, 0, 0))


def swap(x):
    return send_plane(x, lambda c: (0, 0, 1))


def narrow(x, first=None):
    x = x * SHRINK
    if first is not None:
        x = x + 0.0 * first[0, 0]
    return x.astype(jnp.float16)


def widen(x):
    return x.astype(jnp.float32) * (1.0 / SHRINK)


def join_kernel(groups, count, *refs):
    ins, outs = refs[:count], refs[count:]
    for out, group in zip(outs, groups):
        at = 0
        for k in group:
            rows = ins[k].shape[0]
            out[at : at + rows, :] = ins[k][...]
            at += rows


def join(arrays, groups, name, later=()):
    vmem = pl.BlockSpec(memory_space=pltpu.VMEM)
    width = arrays[0].shape[1]
    return pl.pallas_call(
        lambda *refs: join_kernel(
            groups, len(arrays), *refs[: len(arrays)], *refs[len(arrays) + len(later) :]
        ),
        in_specs=[vmem] * len(arrays) + [pl.BlockSpec(memory_space=pl.ANY)] * len(later),
        out_specs=[vmem] * len(groups),
        out_shape=[
            jax.ShapeDtypeStruct((sum(arrays[k].shape[0] for k in g), width), arrays[0].dtype)
            for g in groups
        ],
        compiler_params=pltpu.CompilerParams(vmem_limit_bytes=16 * 1024 * 1024),
        name=name,
    )(*arrays, *later)


def weights_kernel(
    count,
    scale_ref, bias_ref, i0, i1, i2, i3, x0, t1, t2, t3, t4, t5, t6, t7, t8,
    w, img, txt, sem_i, sem_t,
):
    n, width = i0.shape
    own = t1.shape[0]
    mine, other = x0.at[pl.ds(0, own)], x0.at[pl.ds(own, own)]
    texts = (mine, t1, t2, t3, t4, other, t5, t6, t7, t8)
    total, cols = 4 * n, 16 * own
    ins_i = [
        pltpu.make_async_copy(ref, img.at[pl.ds(k * n, n)], sem_i.at[k])
        for k, ref in enumerate((i0, i1, i2, i3))
    ]
    ins_t = []
    at = 0
    for k, ref in enumerate(texts):
        rows = ref.shape[0]
        ins_t.append(
            pltpu.make_async_copy(
                ref, txt.at[pl.ds(at, rows), pl.ds(0, width)], sem_t.at[k]
            )
        )
        at += rows
    for c in ins_i + ins_t:
        c.start()
    txt[:cols, width:] = jnp.zeros((cols, EXTRA), jnp.bfloat16)
    txt[cols:, :width] = jnp.zeros((EXTRA, width), jnp.bfloat16)
    r = lax.broadcasted_iota(jnp.int32, (EXTRA, EXTRA), 0)
    c = lax.broadcasted_iota(jnp.int32, (EXTRA, EXTRA), 1)
    txt[cols:, width:] = jnp.where(r == c, 1.0, 0.0).astype(jnp.bfloat16)
    for c in ins_i + ins_t:
        c.wait()

    scale = scale_ref[0]
    a = scale * LOG2E
    b = bias_ref[0] * LOG2E
    rows = img[...]
    wide = 256
    log_sum = None
    sum_d = None
    sum_dc = None
    for k in range(cols // wide):
        lo, hi = k * wide, (k + 1) * wide
        cosine = lax.dot_general(
            rows, txt[lo:hi, :width], (((1,), (1,)), ((), ())),
            preferred_element_type=jnp.float32,
        )
        e = jnp.exp2(cosine * a + b)
        p = 1.0 + e
        r = pltpu.reciprocal(p, approx=True)
        r = r * (2.0 - p * r)
        d = e * r
        w[:, lo:hi] = (scale * d).astype(jnp.bfloat16)
        q = jnp.log(p[:, :128] * p[:, 128:])
        log_sum = q if log_sum is None else log_sum + q
        dc = d * cosine
        d = jnp.sum((d[:, :128] + d[:, 128:]).reshape(total // 8, 8, 128), axis=0)
        dc = jnp.sum((dc[:, :128] + dc[:, 128:]).reshape(total // 8, 8, 128), axis=0)
        sum_d = d if sum_d is None else sum_d + d
        sum_dc = dc if sum_dc is None else sum_dc + dc
    pairs = count * own
    diagonal = img[:own, :].astype(jnp.float32) * txt[:own, :width].astype(jnp.float32)
    values = (
        jnp.sum(log_sum, axis=1, keepdims=True) * (LIFT / pairs),
        (jnp.sum(sum_dc, keepdims=True) - jnp.sum(diagonal, keepdims=True)) * (LIFT / pairs**2),
        (jnp.sum(sum_d, keepdims=True) - own) * (LIFT / pairs**2),
    )
    lane = lax.broadcasted_iota(jnp.int32, (total, EXTRA), 1)
    side = jnp.zeros((total, EXTRA), jnp.float32)
    for k, value in enumerate(values):
        high = value.astype(jnp.bfloat16).astype(jnp.float32)
        side = jnp.where(lane == 2 * k, high, side)
        side = jnp.where(lane == 2 * k + 1, value - high, side)
    w[:, cols:] = side.astype(jnp.bfloat16)


def weights_block(scale, bias, images, texts):
    n, width = images[0].shape
    rows = 4 * n
    cols = sum(t.shape[0] for t in texts)
    vmem = pl.BlockSpec(memory_space=pltpu.VMEM)
    return pl.pallas_call(
        functools.partial(weights_kernel, NZ * NY * NX * NC),
        in_specs=[pl.BlockSpec(memory_space=pltpu.SMEM)] * 2
        + [pl.BlockSpec(memory_space=pltpu.HBM)] * 13,
        out_specs=[vmem] * 3,
        out_shape=[
            pltpu.VMEM((rows, cols + EXTRA), jnp.bfloat16),
            pltpu.VMEM((rows, width), jnp.bfloat16),
            pltpu.VMEM((cols + EXTRA, width + EXTRA), jnp.bfloat16),
        ],
        scratch_shapes=[pltpu.SemaphoreType.DMA((4,)), pltpu.SemaphoreType.DMA((10,))],
        compiler_params=pltpu.CompilerParams(vmem_limit_bytes=32 * 1024 * 1024),
        name="pair_weights",
    )(scale, bias, *images, *texts)


def normal(ref):
    values = ref[...].astype(jnp.float32)
    inverse = lax.rsqrt(jnp.sum(values * values, axis=1, keepdims=True) + 1e-06)
    return (values * inverse).astype(jnp.bfloat16), inverse


def norm_kernel(i_ref, t_ref, in_ref, tn_ref, ii_ref, ti_ref):
    in_ref[...], ii_ref[...] = normal(i_ref)
    tn_ref[...], ti_ref[...] = normal(t_ref)


def normalize_both(image_emb, text_emb):
    rows, width = image_emb.shape
    vmem = pl.BlockSpec(memory_space=pltpu.VMEM)
    return pl.pallas_call(
        norm_kernel,
        in_specs=[vmem] * 2,
        out_specs=[vmem] * 4,
        out_shape=[jax.ShapeDtypeStruct((rows, width), jnp.bfloat16)] * 2
        + [jax.ShapeDtypeStruct((rows, 1), jnp.float32)] * 2,
        name="normalize",
    )(image_emb, text_emb)


def shard_kernel(tn_ref, o_ref, out):
    own = tn_ref.shape[0]
    out[:own, :] = tn_ref[...]
    out[own:, :] = normal(o_ref)[0]


def chip_shard(text_local, other_emb):
    rows, width = text_local.shape
    vmem = pl.BlockSpec(memory_space=pltpu.VMEM)
    return pl.pallas_call(
        shard_kernel,
        in_specs=[vmem] * 2,
        out_specs=vmem,
        out_shape=jax.ShapeDtypeStruct((2 * rows, width), jnp.bfloat16),
        name="chip_shard",
    )(text_local, other_emb)


def body(image_emb, text_emb, logit_scale, logit_bias):
    scale = logit_scale[0]
    bias = logit_bias[0]
    own = text_emb.shape[0]
    total = own * NZ * NY * NX * NC
    image_local, text_local, image_inv, text_inv = normalize_both(image_emb, text_emb)

    shard = chip_shard(text_local, swap(text_emb))
    ring1 = send_ring(shard, 1)
    near = [image_local] + [send_light(image_local, -i) for i in range(1, 4)]
    (near,) = join(near, [(0, 1, 2, 3)], "join_near")
    images = [near] + [send_heavy(near, -i) for i in (1, 3, 2)]
    images = [images[0], images[1], images[3], images[2]]
    ring2 = send_ring(ring1, 1)
    ring3 = send_ring(ring2, 1)
    ring4 = send_ring(ring3[:own], 1)
    (last,) = join([ring4], [(0,)], "join_last", [images[3], images[2]])
    w, img, txt = weights_block(
        logit_scale, logit_bias, images,
        [shard, ring4, ring1, ring2, swap(ring3)]
        + [swap(last), swap(ring1), swap(ring2), ring3],
    )

    width = text_emb.shape[1]
    n = own * NZ
    m = 4 * own
    contract = (((0,), (0,)), ((), ()))
    theirs = lax.dot_general(w[:, n : 2 * n], img, contract, preferred_element_type=jnp.float32)
    theirs = swap(narrow(theirs))

    def heavy(i, first=None):
        part = jnp.dot(w[i * m : (i + 1) * m], txt, preferred_element_type=jnp.float32)
        return send_heavy(narrow(part, first), i)

    got = [heavy(1)]
    gt = lax.dot_general(w[:, :n], img, contract, preferred_element_type=jnp.float32)
    gt = gt + widen(theirs)
    back2 = send_ring(narrow(gt[m:]), -1)
    near4 = widen(back2[3 * own :]) + widen(swap(back2[2 * own : 3 * own]))
    near4 = near4 + gt[own : 2 * own]
    back_far = send_z(narrow(near4), 4)
    got += [heavy(3), heavy(2, gt)]
    back1 = send_ring(narrow(gt[2 * own : m] + widen(back2[: 2 * own])), -1)
    text_share = gt[:own] + widen(back_far) + widen(back1[:own]) + widen(swap(back1[own:]))

    part = jnp.dot(w[:m], txt, preferred_element_type=jnp.float32)
    for g in got:
        part = part + widen(g)
    groups = [
        [(z * NY * NX + y * NX + g) * NC for z in range(NZ) for y in range(NY)]
        + [(z * NY * NX + g * NX + x) * NC + 1 for z in range(NZ) for x in range(NX)]
        for g in range(NX)
    ]
    sums = part[None, :1, width:] + 0.0 * near4[0, 0]
    sums = jnp.broadcast_to(sums, (len(groups[0]), 1, EXTRA))
    sums = lax.all_to_all(sums, ("row", "col"), 0, 0, axis_index_groups=groups)
    sums = jnp.sum(sums, axis=0)[0] * (1.0 / LIFT)
    scalar_grads = lax.slice(sums, (2,), (6,), (2,)) + lax.slice(sums, (3,), (7,), (2,))
    image_share = part[:own]
    for i in range(1, 4):
        image_share = image_share + widen(
            send_light(narrow(part[i * own : (i + 1) * own]), i)
        )
    side = image_share[:, width:] * (1.0 / LIFT)
    image_share = image_share[:, :width]
    loss_sum = side[:, 0] + side[:, 1]
    image_f = image_local.astype(jnp.float32)
    text_f = text_local.astype(jnp.float32)
    cosine = jnp.sum(image_f * text_f, axis=1, keepdims=True)
    logits = scale * cosine + bias
    d = jax.nn.sigmoid(logits)
    w_plain = lax.reduce_precision(scale * d, 8, 7)
    w_right = lax.reduce_precision(scale * -jax.nn.sigmoid(-logits), 8, 7)
    fix = w_right - w_plain
    image_share = image_share + fix * text_f
    text_share = text_share + fix * image_f
    loss_rows = loss_sum - logits[:, 0] / total
    image_unit = image_emb.astype(jnp.float32) * image_inv
    text_unit = text_emb.astype(jnp.float32) * text_inv
    text_grad = text_inv * (
        text_share - text_unit * jnp.sum(text_unit * text_share, axis=1, keepdims=True)
    )
    image_grad = image_inv * (
        image_share - image_unit * jnp.sum(image_unit * image_share, axis=1, keepdims=True)
    )
    return (loss_rows, image_grad, text_grad, scalar_grads)


def solution(mesh):
    return jax.shard_map(
        body,
        mesh=mesh,
        in_specs=(P(("row", "col"), None), P(("row", "col"), None), P(), P()),
        out_specs=(P(("row", "col")), P(("row", "col"), None), P(("row", "col"), None), P()),
        check_vma=False,
    )
```

```python
import functools
import math
import jax
import jax.numpy as jnp
from jax import lax
from jax.experimental import pallas as pl
from jax.experimental.pallas import tpu as pltpu
from jax.sharding import PartitionSpec as P

NZ, NY, NX, NC = 8, 4, 4, 2
SHRINK = 0.125
LOG2E = 1.0 / math.log(2.0)
EXTRA = 128
LIFT = 1024.0


def send_z(x, d):
    return lax.ppermute(x, "row", [(i, (i + d) % NZ) for i in range(NZ)])


def send_ring(x, d):
    pairs = []
    for z in range(NZ):
        for s in range(NY * NX):
            for c in range(NC):
                to = (z + (d if c == 0 else -d)) % NZ
                pairs.append(((z * NY * NX + s) * NC + c, (to * NY * NX + s) * NC + c))
    return lax.ppermute(x, ("row", "col"), pairs)


def send_plane(x, move):
    pairs = []
    for y in range(NY):
        for x_ in range(NX):
            for c in range(NC):
                dy, dx, dc = move(c)
                src = (y * NX + x_) * NC + c
                dst = (((y + dy) % NY) * NX + (x_ + dx) % NX) * NC + (c + dc) % NC
                pairs.append((src, dst))
    return lax.ppermute(x, "col", pairs)


def send_light(x, i):
    return send_plane(x, lambda c: (i, 0, 0) if c == 0 else (0, i, 0))


def send_heavy(x, i):
    return send_plane(x, lambda c: (0, i, 0) if c == 0 else (i, 0, 0))


def swap(x):
    return send_plane(x, lambda c: (0, 0, 1))


def narrow(x, first=None):
    x = x * SHRINK
    if first is not None:
        x = x + 0.0 * first[0, 0]
    return x.astype(jnp.float16)


def widen(x):
    return x.astype(jnp.float32) * (1.0 / SHRINK)


def join_kernel(groups, count, *refs):
    ins, outs = refs[:count], refs[count:]
    for out, group in zip(outs, groups):
        at = 0
        for k in group:
            rows = ins[k].shape[0]
            out[at : at + rows, :] = ins[k][...]
            at += rows


def join(arrays, groups, name, later=()):
    vmem = pl.BlockSpec(memory_space=pltpu.VMEM)
    width = arrays[0].shape[1]
    return pl.pallas_call(
        lambda *refs: join_kernel(
            groups, len(arrays), *refs[: len(arrays)], *refs[len(arrays) + len(later) :]
        ),
        in_specs=[vmem] * len(arrays) + [pl.BlockSpec(memory_space=pl.ANY)] * len(later),
        out_specs=[vmem] * len(groups),
        out_shape=[
            jax.ShapeDtypeStruct((sum(arrays[k].shape[0] for k in g), width), arrays[0].dtype)
            for g in groups
        ],
        compiler_params=pltpu.CompilerParams(vmem_limit_bytes=16 * 1024 * 1024),
        name=name,
    )(*arrays, *later)


def weights_kernel(
    count,
    scale_ref, bias_ref, i0, i1, i2, i3, x0, t1, t2, t3, t4, t5, t6, t7, t8,
    w, img, txt, sem_i, sem_t,
):
    n, width = i0.shape
    own = t1.shape[0]
    mine, other = x0.at[pl.ds(0, own)], x0.at[pl.ds(own, own)]
    texts = (mine, t1, t2, t3, t4, other, t5, t6, t7, t8)
    total, cols = 4 * n, 16 * own
    ins_i = [
        pltpu.make_async_copy(ref, img.at[pl.ds(k * n, n)], sem_i.at[k])
        for k, ref in enumerate((i0, i1, i2, i3))
    ]
    ins_t = []
    at = 0
    for k, ref in enumerate(texts):
        rows = ref.shape[0]
        ins_t.append(
            pltpu.make_async_copy(
                ref, txt.at[pl.ds(at, rows), pl.ds(0, width)], sem_t.at[k]
            )
        )
        at += rows
    for c in ins_i + ins_t:
        c.start()
    txt[:cols, width:] = jnp.zeros((cols, EXTRA), jnp.bfloat16)
    txt[cols:, :width] = jnp.zeros((EXTRA, width), jnp.bfloat16)
    r = lax.broadcasted_iota(jnp.int32, (EXTRA, EXTRA), 0)
    c = lax.broadcasted_iota(jnp.int32, (EXTRA, EXTRA), 1)
    txt[cols:, width:] = jnp.where(r == c, 1.0, 0.0).astype(jnp.bfloat16)
    for c in ins_i + ins_t:
        c.wait()

    scale = scale_ref[0]
    a = scale * LOG2E
    b = bias_ref[0] * LOG2E
    rows = img[...]
    wide = 256
    log_sum = None
    sum_d = None
    sum_dc = None
    for k in range(cols // wide):
        lo, hi = k * wide, (k + 1) * wide
        cosine = lax.dot_general(
            rows, txt[lo:hi, :width], (((1,), (1,)), ((), ())),
            preferred_element_type=jnp.float32,
        )
        e = jnp.exp2(cosine * a + b)
        p = 1.0 + e
        r = pltpu.reciprocal(p, approx=True)
        r = r * (2.0 - p * r)
        d = e * r
        w[:, lo:hi] = (scale * d).astype(jnp.bfloat16)
        q = jnp.log(p[:, :128] * p[:, 128:])
        log_sum = q if log_sum is None else log_sum + q
        dc = d * cosine
        d = jnp.sum((d[:, :128] + d[:, 128:]).reshape(total // 8, 8, 128), axis=0)
        dc = jnp.sum((dc[:, :128] + dc[:, 128:]).reshape(total // 8, 8, 128), axis=0)
        sum_d = d if sum_d is None else sum_d + d
        sum_dc = dc if sum_dc is None else sum_dc + dc
    pairs = count * own
    diagonal = img[:own, :].astype(jnp.float32) * txt[:own, :width].astype(jnp.float32)
    values = (
        jnp.sum(log_sum, axis=1, keepdims=True) * (LIFT / pairs),
        (jnp.sum(sum_dc, keepdims=True) - jnp.sum(diagonal, keepdims=True)) * (LIFT / pairs**2),
        (jnp.sum(sum_d, keepdims=True) - own) * (LIFT / pairs**2),
    )
    lane = lax.broadcasted_iota(jnp.int32, (total, EXTRA), 1)
    side = jnp.zeros((total, EXTRA), jnp.float32)
    for k, value in enumerate(values):
        high = value.astype(jnp.bfloat16).astype(jnp.float32)
        side = jnp.where(lane == 2 * k, high, side)
        side = jnp.where(lane == 2 * k + 1, value - high, side)
    w[:, cols:] = side.astype(jnp.bfloat16)


def weights_block(scale, bias, images, texts):
    n, width = images[0].shape
    rows = 4 * n
    cols = sum(t.shape[0] for t in texts)
    vmem = pl.BlockSpec(memory_space=pltpu.VMEM)
    return pl.pallas_call(
        functools.partial(weights_kernel, NZ * NY * NX * NC),
        in_specs=[pl.BlockSpec(memory_space=pltpu.SMEM)] * 2
        + [pl.BlockSpec(memory_space=pltpu.HBM)] * 13,
        out_specs=[vmem] * 3,
        out_shape=[
            pltpu.VMEM((rows, cols + EXTRA), jnp.bfloat16),
            pltpu.VMEM((rows, width), jnp.bfloat16),
            pltpu.VMEM((cols + EXTRA, width + EXTRA), jnp.bfloat16),
        ],
        scratch_shapes=[pltpu.SemaphoreType.DMA((4,)), pltpu.SemaphoreType.DMA((10,))],
        compiler_params=pltpu.CompilerParams(vmem_limit_bytes=32 * 1024 * 1024),
        name="pair_weights",
    )(scale, bias, *images, *texts)


def normal(ref):
    values = ref[...].astype(jnp.float32)
    inverse = lax.rsqrt(jnp.sum(values * values, axis=1, keepdims=True) + 1e-06)
    return (values * inverse).astype(jnp.bfloat16), inverse


def norm_kernel(i_ref, t_ref, o_ref, in_ref, shard_ref, ii_ref, ti_ref):
    own = t_ref.shape[0]
    in_ref[...], ii_ref[...] = normal(i_ref)
    shard_ref[:own, :], ti_ref[...] = normal(t_ref)
    shard_ref[own:, :] = normal(o_ref)[0]


def normalize_all(image_emb, text_emb, other_emb):
    rows, width = image_emb.shape
    vmem = pl.BlockSpec(memory_space=pltpu.VMEM)
    return pl.pallas_call(
        norm_kernel,
        in_specs=[vmem] * 3,
        out_specs=[vmem] * 4,
        out_shape=[
            jax.ShapeDtypeStruct((rows, width), jnp.bfloat16),
            jax.ShapeDtypeStruct((2 * rows, width), jnp.bfloat16),
            jax.ShapeDtypeStruct((rows, 1), jnp.float32),
            jax.ShapeDtypeStruct((rows, 1), jnp.float32),
        ],
        name="normalize",
    )(image_emb, text_emb, other_emb)


def body(image_emb, text_emb, logit_scale, logit_bias):
    scale = logit_scale[0]
    bias = logit_bias[0]
    own = text_emb.shape[0]
    total = own * NZ * NY * NX * NC
    image_local, shard, image_inv, text_inv = normalize_all(image_emb, text_emb, swap(text_emb))

    ring1 = send_ring(shard, 1)
    near = [image_local] + [send_light(image_local, -i) for i in range(1, 4)]
    (near,) = join(near, [(0, 1, 2, 3)], "join_near")
    images = [near] + [send_heavy(near, -i) for i in (1, 3, 2)]
    images = [images[0], images[1], images[3], images[2]]
    ring2 = send_ring(ring1, 1)
    ring3 = send_ring(ring2, 1)
    ring4 = send_ring(ring3[:own], 1)
    (last,) = join([ring4], [(0,)], "join_last", [images[3], images[2]])
    w, img, txt = weights_block(
        logit_scale, logit_bias, images,
        [shard, ring4, ring1, ring2, swap(ring3)]
        + [swap(last), swap(ring1), swap(ring2), ring3],
    )

    width = text_emb.shape[1]
    n = own * NZ
    m = 4 * own
    contract = (((0,), (0,)), ((), ()))
    theirs = lax.dot_general(w[:, n : 2 * n], img, contract, preferred_element_type=jnp.float32)
    theirs = swap(narrow(theirs))

    def heavy(i, first=None):
        part = jnp.dot(w[i * m : (i + 1) * m], txt, preferred_element_type=jnp.float32)
        return send_heavy(narrow(part, first), i)

    got = [heavy(1)]
    gt = lax.dot_general(w[:, :n], img, contract, preferred_element_type=jnp.float32)
    gt = gt + widen(theirs)
    back2 = send_ring(narrow(gt[m:]), -1)
    near4 = widen(back2[3 * own :]) + widen(swap(back2[2 * own : 3 * own]))
    near4 = near4 + gt[own : 2 * own]
    back_far = send_z(narrow(near4), 4)
    got += [heavy(3), heavy(2, gt)]
    back1 = send_ring(narrow(gt[2 * own : m] + widen(back2[: 2 * own])), -1)
    text_share = gt[:own] + widen(back_far) + widen(back1[:own]) + widen(swap(back1[own:]))

    part = jnp.dot(w[:m], txt, preferred_element_type=jnp.float32)
    for g in got:
        part = part + widen(g)
    groups = [
        [(z * NY * NX + y * NX + g) * NC for z in range(NZ) for y in range(NY)]
        + [(z * NY * NX + g * NX + x) * NC + 1 for z in range(NZ) for x in range(NX)]
        for g in range(NX)
    ]
    sums = part[None, :1, width:] + 0.0 * near4[0, 0]
    sums = jnp.broadcast_to(sums, (len(groups[0]), 1, EXTRA))
    sums = lax.all_to_all(sums, ("row", "col"), 0, 0, axis_index_groups=groups)
    sums = jnp.sum(sums, axis=0)[0] * (1.0 / LIFT)
    scalar_grads = lax.slice(sums, (2,), (6,), (2,)) + lax.slice(sums, (3,), (7,), (2,))
    image_share = part[:own]
    for i in range(1, 4):
        image_share = image_share + widen(
            send_light(narrow(part[i * own : (i + 1) * own]), i)
        )
    side = image_share[:, width:] * (1.0 / LIFT)
    image_share = image_share[:, :width]
    loss_sum = side[:, 0] + side[:, 1]
    image_f = image_local.astype(jnp.float32)
    text_f = shard[:own].astype(jnp.float32)
    cosine = jnp.sum(image_f * text_f, axis=1, keepdims=True)
    logits = scale * cosine + bias
    d = jax.nn.sigmoid(logits)
    w_plain = lax.reduce_precision(scale * d, 8, 7)
    w_right = lax.reduce_precision(scale * -jax.nn.sigmoid(-logits), 8, 7)
    fix = w_right - w_plain
    image_share = image_share + fix * text_f
    text_share = text_share + fix * image_f
    loss_rows = loss_sum - logits[:, 0] / total
    image_unit = image_emb.astype(jnp.float32) * image_inv
    text_unit = text_emb.astype(jnp.float32) * text_inv
    text_grad = text_inv * (
        text_share - text_unit * jnp.sum(text_unit * text_share, axis=1, keepdims=True)
    )
    image_grad = image_inv * (
        image_share - image_unit * jnp.sum(image_unit * image_share, axis=1, keepdims=True)
    )
    return (loss_rows, image_grad, text_grad, scalar_grads)


def solution(mesh):
    return jax.shard_map(
        body,
        mesh=mesh,
        in_specs=(P(("row", "col"), None), P(("row", "col"), None), P(), P()),
        out_specs=(P(("row", "col")), P(("row", "col"), None), P(("row", "col"), None), P()),
        check_vma=False,
    )
```
